32 devices in a mesh: seq: 2 (over x), chan: 16 (over z, y, core).
Axes of the slice: x: 2, y: 2, z: 4, core: 2. Of those that a mesh axis runs over, the one named last changes fastest.
Arguments:
- tokens: bfloat16 [2048, 4096], P('seq', 'chan'), may hold values from -6 to 6
- in_weight: bfloat16 [4096, 3, 4096], P(None, None, 'chan'), may hold values from -0.09375 to 0.09375
- short_taps: float32 [3, 3, 4096], P(None, None, 'chan'), may hold values from -3 to 3
- filter_taps: float32 [2048, 4096], P('seq', 'chan'), may hold values from -1 to 1
- skip_gain: float32 [4096], P('chan'), may hold values from -4 to 4
- out_weight: bfloat16 [4096, 4096], P('chan'), may hold values from -0.125 to 0.125
Outputs:
- layer_out: bfloat16 [2048, 4096], P('seq', 'chan')
The draws below stay inside these ranges and needn't reach their ends.
All inputs are finite; a program needn't handle non-finite values.
Results may differ from the reference program's by a relative error of at most 0.007.
Values may be sent and summed in bfloat16 or wider, within the bound.
A program may use at most 128 MiB of HBM per device.

```python
import math
import jax
import jax.numpy as jnp

EMBED_DIMENSION = 4096
STEP_COUNT = 2048


def draw_filter_taps(key, part):
    derived_prng_streams = jax.random.split(key, 6)
    element_ordinal = jnp.arange(STEP_COUNT, dtype=jnp.float32)[:, None]
    quick_share = 0.5
    quick_mask = jax.random.uniform(derived_prng_streams[0], (1, EMBED_DIMENSION)) < quick_share
    quick_span = jax.random.uniform(derived_prng_streams[1], (1, EMBED_DIMENSION), minval=30.0, maxval=50.0)
    slow_span = STEP_COUNT * jnp.exp(jax.random.uniform(derived_prng_streams[2], (1, EMBED_DIMENSION), minval=math.log(2.0), maxval=math.log(6.0)))
    decay_span = jnp.where(quick_mask, quick_span, slow_span)
    impulse_start = jax.random.randint(derived_prng_streams[3], (3, EMBED_DIMENSION), 0, STEP_COUNT).astype(jnp.float32)
    impulse_keep_mask = jax.random.uniform(derived_prng_streams[4], (3, EMBED_DIMENSION), minval=0.6, maxval=0.8)
    scaling_coefficient = jnp.ones((STEP_COUNT, EMBED_DIMENSION), jnp.float32)
    for impulse_signal in range(3):
        scaling_coefficient = scaling_coefficient * jnp.where(element_ordinal >= impulse_start[impulse_signal][None, :], impulse_keep_mask[impulse_signal][None, :], 1.0)
    envelope = jnp.exp(-element_ordinal / decay_span) * scaling_coefficient / jnp.sqrt(jnp.minimum(decay_span, float(STEP_COUNT)))
    rough_part = jnp.clip(jax.random.normal(derived_prng_streams[5], (STEP_COUNT, EMBED_DIMENSION)), -4.0, 4.0)
    return (envelope * rough_part).astype(jnp.float32)


def raised(drawn, stream_key, source, target, blocks, factor):
    def block_of(dim):
        return (jnp.arange(drawn.shape[dim]) // (drawn.shape[dim] // blocks)).reshape((-1,) + (1,) * (drawn.ndim - 1 - dim))

    first = jax.random.permutation(stream_key, blocks)[block_of(target)]
    other_side = (block_of(target) + blocks // 2) % blocks
    return jnp.where((block_of(source) == first) | (block_of(source) == other_side), factor * drawn, drawn)


def block_levels(stream_key, extent, cuts, low, high):
    def one(axis_at, shards_of):
        steps = jax.random.uniform(jax.random.fold_in(jax.random.fold_in(stream_key, 6), axis_at), (shards_of,), jnp.float32, low / len(cuts), high / len(cuts))
        return jnp.repeat(jnp.exp(steps), extent[axis_at] // shards_of).reshape((-1,) + (1,) * (len(extent) - axis_at - 1))

    gain = one(*cuts[0])
    for cut in cuts[1:]:
        gain = gain * one(*cut)
    return gain


def centred(key, shape, deviation, most, cuts=(), kind=jnp.bfloat16):
    array = deviation * jax.random.normal(key, shape, jnp.float32)
    if cuts:
        array = array * block_levels(key, shape, cuts, -0.22, 0.18)
    return jnp.clip(array, -most, most).astype(kind)


def bell_draw_with(own_key, shape, deviation, reach, cuts, heavy, kind=jnp.bfloat16):
    array = deviation * jax.random.normal(own_key, shape, jnp.float32)
    if cuts:
        array = array * block_levels(own_key, shape, cuts, -0.22, 0.18)
    return jnp.clip(raised(array, jax.random.fold_in(own_key, 3), *heavy), -reach, reach).astype(kind)


def setup_inputs(seed: int = 0) -> dict:
    seeds = jax.random.split(jax.random.key(seed), 7)
    tokens = centred(seeds[0], (STEP_COUNT, EMBED_DIMENSION), 1.0, 6.0, ((0, 2), (1, 16)))
    in_weight = centred(seeds[1], (EMBED_DIMENSION, 3, EMBED_DIMENSION), EMBED_DIMENSION ** -0.5, 0.09375, ((2, 16),))
    short_taps = centred(seeds[2], (3, 3, EMBED_DIMENSION), 0.6, 3.0, ((2, 16),), jnp.float32)
    filter_taps = draw_filter_taps(jax.random.fold_in(seeds[6], 71), 0)
    skip_gain = centred(seeds[4], (EMBED_DIMENSION,), 1.0, 4.0, ((0, 16),), jnp.float32)
    out_weight = bell_draw_with(seeds[5], (EMBED_DIMENSION, EMBED_DIMENSION), EMBED_DIMENSION ** -0.5, 0.125, ((0, 16),), (0, 1, 16, 2.0))
    return {"tokens": tokens, "in_weight": in_weight, "short_taps": short_taps, "filter_taps": filter_taps, "skip_gain": skip_gain, "out_weight": out_weight}


def reference(tokens, in_weight, short_taps, filter_taps, skip_gain, out_weight):
    projected = jnp.dot(tokens, in_weight.reshape(EMBED_DIMENSION, 3 * EMBED_DIMENSION), preferred_element_type=jnp.float32)
    projected = projected.astype(jnp.bfloat16).reshape(STEP_COUNT, 3, EMBED_DIMENSION).astype(jnp.float32)
    padded = jnp.pad(projected, ((2, 0), (0, 0), (0, 0)))
    mixed = short_taps[0] * padded[2:] + short_taps[1] * padded[1:-1] + short_taps[2] * padded[:-2]
    gate_out = mixed[:, 0]
    signal = mixed[:, 1] * mixed[:, 2]
    block_width = max(EMBED_DIMENSION // 8, 1)
    pieces = []
    for block_start in range(0, EMBED_DIMENSION, block_width):
        signal_block = signal[:, block_start:block_start + block_width]
        filter_block = filter_taps[:, block_start:block_start + block_width]
        spectrum = jnp.fft.rfft(signal_block, n=2 * STEP_COUNT, axis=0) * jnp.fft.rfft(filter_block, n=2 * STEP_COUNT, axis=0)
        pieces.append(jnp.fft.irfft(spectrum, n=2 * STEP_COUNT, axis=0)[:STEP_COUNT])
    convolved = jnp.concatenate(pieces, axis=1)
    hidden = (gate_out * (convolved + skip_gain * signal)).astype(jnp.bfloat16)
    return jnp.dot(hidden, out_weight, preferred_element_type=jnp.float32).astype(jnp.bfloat16)
```

```python
import functools
import math

import jax
import jax.numpy as jnp
import numpy as np
from jax import lax
from jax.experimental import pallas as pl
from jax.experimental.pallas import tpu as pltpu
from jax.sharding import PartitionSpec as P

MESH = pl.DeviceIdType.MESH
BF = jnp.bfloat16
F32 = jnp.float32
HALO = 16


def split_pair(array):
    high = array.astype(np.float32).astype(BF)
    low = (array - high.astype(np.float64)).astype(np.float32).astype(BF)
    return np.stack([np.asarray(high), np.asarray(low)])


def forward_matrix(block):
    angle = math.pi * (2 * np.arange(block)[:, None] + 1) * np.arange(block)[None, :] / (2 * block)
    return split_pair(np.concatenate([np.cos(angle), -np.sin(angle)], axis=0))


def inverse_matrix(block):
    place = block + np.arange(block)[:, None]
    angle = math.pi * place * (2 * np.arange(block)[None, :] + 1) / (2 * block)
    return split_pair(np.concatenate([np.cos(angle), -np.sin(angle)], axis=1) / block)


def dot(a, b):
    return jnp.dot(a, b, preferred_element_type=F32)


def remote(src, dst, send, recv, where):
    return pltpu.make_async_remote_copy(
        src_ref=src, dst_ref=dst, send_sem=send, recv_sem=recv, device_id=where, device_id_type=MESH
    )


def greet(devices):
    barrier = pltpu.get_barrier_semaphore()
    total = 0
    for where, exists in devices:
        if exists is None:
            pl.semaphore_signal(barrier, inc=1, device_id=where, device_id_type=MESH)
            total = total + 1
        else:

            @pl.when(exists)
            def _():
                pl.semaphore_signal(barrier, inc=1, device_id=where, device_id_type=MESH)

            total = total + exists.astype(jnp.int32)
    pl.semaphore_wait(barrier, total)


def position(chans):
    me = lax.axis_index("chan")
    far = chans // 4
    return me, me // 4, (me // 2) % 2, me % 2, far


def chan_peers(chans):
    me, zi, yi, ci, far = position(chans)
    core = {"chan": me + 1 - 2 * ci}
    side = {"chan": me + 2 - 4 * yi}
    up = {"chan": jnp.minimum(me + 4, chans - 1)}
    down = {"chan": jnp.maximum(me - 4, 0)}
    return core, side, up, down


def seq_peers(seqs):
    mine = lax.axis_index("seq")
    return mine, [{"seq": lax.rem(mine + k, seqs)} for k in range(1, seqs)]


def gather_kernel(
    seqs, chans, tok, weight, taps, fwd, proj, window,
    buf, acc, stage, whole, spec,
    zsend, zrecv, ysend, yrecv, csend, crecv, fsend, frecv,
):
    me, zi, yi, ci, far = position(chans)
    core, side, up, down = chan_peers(chans)
    mine, peers = seq_peers(seqs)
    rows, width = tok.shape
    narrow = taps.shape[1] // seqs
    block = fwd.shape[2]
    has_up, has_down = zi < far - 1, zi > 0
    greet([(core, None), (side, None), (up, has_up), (down, has_down)] + [(p, None) for p in peers])

    def send_up(src, z):
        return remote(src, buf.at[z * 4 + yi * 2 + ci], zsend.at[0, z], zrecv.at[z], up)

    def send_down(src, z):
        return remote(src, buf.at[z * 4 + yi * 2 + ci], zsend.at[1, z], zrecv.at[z], down)

    def send_side(src, z):
        return remote(src, buf.at[z * 4 + yi * 2 + ci], ysend.at[z], yrecv.at[z], side)

    def send_core(src, y, z):
        return remote(src, buf.at[z * 4 + y * 2 + ci], csend.at[y * far + z], crecv.at[y * far + z], core)

    def slot(z, y, c):
        return buf.at[z * 4 + y * 2 + c]

    def add(src, ident):
        part = weight[pl.ds(pl.multiple_of(ident * width, width), width), :]
        tile = min(rows, 256)

        @pl.loop(0, rows // tile)
        def _(r):
            at = pl.ds(pl.multiple_of(r * tile, tile), tile)
            acc[at, :] += dot(src[at, :], part)

    @pl.when(has_up)
    def _():
        send_up(tok, zi).start()

    @pl.when(has_down)
    def _():
        send_down(tok, zi).start()

    send_side(tok, zi).start()
    send_core(tok, yi, zi).start()

    for j in range(seqs):
        stage[j] = taps[:, j * narrow:(j + 1) * narrow]

    def filter_copy(k):
        to = lax.rem(mine + k, seqs)
        return remote(stage.at[to], whole.at[mine], fsend.at[k], frecv.at[k], {"seq": to})

    for k in range(1, seqs):
        filter_copy(k).start()
    whole[pl.ds(mine, 1)] = stage[pl.ds(mine, 1)]

    acc[...] = jnp.zeros_like(acc)
    add(tok, me)

    def from_side(z):
        here = slot(z, 1 - yi, ci)
        remote(here, here, ysend.at[z], yrecv.at[z], side).wait_recv()
        send_core(here, 1 - yi, z).start()
        add(here, z * 4 + (1 - yi) * 2 + ci)

    def from_core(y, z):
        here = slot(z, y, 1 - ci)
        remote(here, here, csend.at[y * far + z], crecv.at[y * far + z], core).wait_recv()
        add(here, z * 4 + y * 2 + 1 - ci)

    def far_in(z, going_up):
        here = slot(z, yi, ci)
        remote(here, here, zsend.at[0, z], zrecv.at[z], up).wait_recv()
        if going_up:

            @pl.when(has_up)
            def _():
                send_up(here, z).start()
        else:

            @pl.when(has_down)
            def _():
                send_down(here, z).start()

        send_side(here, z).start()
        send_core(here, yi, z).start()
        add(here, z * 4 + yi * 2 + ci)

    @pl.loop(1, far)
    def _(s):
        @pl.when(zi - s >= 0)
        def _():
            far_in(zi - s, True)

        @pl.when(zi + s < far)
        def _():
            far_in(zi + s, False)

        @pl.when(zi - s + 1 >= 0)
        def _():
            from_side(zi - s + 1)
            from_core(yi, zi - s + 1)

        @pl.when(jnp.logical_and(zi + s - 1 < far, s > 1))
        def _():
            from_side(zi + s - 1)
            from_core(yi, zi + s - 1)

    for k in range(1, seqs):
        came = lax.rem(mine - k + seqs, seqs)
        remote(stage.at[came], whole.at[came], fsend.at[k], frecv.at[k], {"seq": came}).wait_recv()
    per = rows // block
    count = seqs * per

    @pl.loop(0, count)
    def _(p):
        x = whole[p // per, pl.ds(pl.multiple_of((p % per) * block, block), block), :]
        high = x.astype(BF)
        low = (x - high.astype(F32)).astype(BF)
        spec[p] = dot(fwd[0], high) + (dot(fwd[0], low) + dot(fwd[1], high))

    parity = lax.broadcasted_iota(jnp.int32, (block, narrow), 0) % 2
    sign = (1 - 2 * parity).astype(F32)

    @pl.loop(0, count)
    def _(p):
        keep = jnp.where(p > 0, 1.0, 0.0).astype(F32)
        before = jnp.maximum(p - 1, 0)
        window[p, :block, :] = keep * spec[before, :block, :] + sign * spec[p, block:, :]
        window[p, block:, :] = keep * spec[before, block:, :] - sign * spec[p, :block, :]

    @pl.when(zi - far + 1 >= 0)
    def _():
        from_side(zi - far + 1)
        from_core(yi, zi - far + 1)

    @pl.when(zi + far - 1 < far)
    def _():
        from_side(zi + far - 1)
        from_core(yi, zi + far - 1)

    @pl.loop(0, far)
    def _(k):
        from_core(1 - yi, lax.rem(zi + k, far))

    proj[...] = acc[...].astype(BF)

    @pl.when(has_up)
    def _():
        @pl.loop(0, far)
        def _(z):
            @pl.when(z <= zi)
            def _():
                send_up(tok, z).wait_send()

    @pl.when(has_down)
    def _():
        @pl.loop(0, far)
        def _(z):
            @pl.when(z >= zi)
            def _():
                send_down(tok, z).wait_send()

    @pl.loop(0, far)
    def _(z):
        send_side(tok, z).wait_send()
        send_core(tok, 0, z).wait_send()
        send_core(tok, 1, z).wait_send()

    for k in range(1, seqs):
        filter_copy(k).wait_send()


def mix_kernel(
    seqs, proj, short, skip, fwd, inv, window, hidden,
    ext, edge, signal, gate, stage, whole, spec, prod, back, done,
    hsend, hrecv, ssend, srecv, bsend, brecv,
):
    mine, peers = seq_peers(seqs)
    rows = proj.shape[0]
    chan = proj.shape[1] // 3
    narrow = chan // seqs
    block = fwd.shape[2]
    per = rows // block
    count = seqs * per
    greet([(p, None) for p in peers])
    has_next, has_before = mine < seqs - 1, mine > 0
    following = {"seq": jnp.minimum(mine + 1, seqs - 1)}
    halo = remote(proj.at[pl.ds(rows - HALO, HALO)], edge, hsend, hrecv, following)

    @pl.when(has_next)
    def _():
        halo.start()

    ext[HALO:, :] = proj[...].astype(F32)

    @pl.when(has_before)
    def _():
        halo.wait_recv()
        ext[:HALO, :] = edge[...].astype(F32)

    @pl.when(jnp.logical_not(has_before))
    def _():
        ext[:HALO, :] = jnp.zeros((HALO, 3 * chan), F32)

    tile = min(rows, 128)
    for r in range(rows // tile):
        at = HALO + r * tile

        def mixed(g):
            cols = slice(g * chan, (g + 1) * chan)
            return (
                short[g:g + 1, :] * ext[at:at + tile, cols]
                + short[3 + g:4 + g, :] * ext[at - 1:at - 1 + tile, cols]
                + short[6 + g:7 + g, :] * ext[at - 2:at - 2 + tile, cols]
            )

        gate[r * tile:(r + 1) * tile, :] = mixed(0)
        value = mixed(1) * mixed(2)
        signal[r * tile:(r + 1) * tile, :] = value
        for j in range(seqs):
            stage[j, r * tile:(r + 1) * tile, :] = value[:, j * narrow:(j + 1) * narrow].astype(BF)

    def signal_copy(k):
        to = lax.rem(mine + k, seqs)
        return remote(stage.at[to], whole.at[mine], ssend.at[k], srecv.at[k], {"seq": to})

    for k in range(1, seqs):
        signal_copy(k).start()
    whole[pl.ds(mine, 1)] = stage[pl.ds(mine, 1)]

    def transform(owner):
        @pl.loop(0, per)
        def _(q):
            x = whole[owner, pl.ds(pl.multiple_of(q * block, block), block), :]
            spec[owner * per + q] = dot(fwd[0], x) + dot(fwd[1], x)

    transform(mine)
    for k in range(1, seqs):
        came = lax.rem(mine - k + seqs, seqs)
        remote(stage.at[came], whole.at[came], ssend.at[k], srecv.at[k], {"seq": came}).wait_recv()
        transform(came)

    @pl.loop(0, block // 8)
    def _(r):
        real = pl.ds(pl.multiple_of(r * 8, 8), 8)
        imag = pl.ds(pl.multiple_of(block + r * 8, 8), 8)
        for k in range(count):
            re = im = None
            for j in range(k + 1):
                a, b = spec[j, real, :], spec[j, imag, :]
                c, d = window[k - j, real, :], window[k - j, imag, :]
                one, two = a * c - b * d, a * d + b * c
                re = one if re is None else re + one
                im = two if im is None else im + two
            prod[k, real, :] = re
            prod[k, imag, :] = im

    def invert(owner):
        @pl.loop(0, per)
        def _(q):
            x = prod[owner * per + q]
            high = x.astype(BF)
            low = (x - high.astype(F32)).astype(BF)
            y = dot(inv[0], high) + (dot(inv[0], low) + dot(inv[1], high))
            back[owner, pl.ds(pl.multiple_of(q * block, block), block), :] = y.astype(BF)

    def back_copy(k):
        to = lax.rem(mine + k, seqs)
        return remote(back.at[to], done.at[mine], bsend.at[k], brecv.at[k], {"seq": to})

    for k in range(1, seqs):
        invert(lax.rem(mine + k, seqs))
        back_copy(k).start()
    invert(mine)
    done[pl.ds(mine, 1)] = back[pl.ds(mine, 1)]
    for k in range(1, seqs):
        came = lax.rem(mine - k + seqs, seqs)
        remote(back.at[came], done.at[came], bsend.at[k], brecv.at[k], {"seq": came}).wait_recv()

    for j in range(seqs):
        cols = slice(j * narrow, (j + 1) * narrow)
        for r in range(rows // tile):
            at = slice(r * tile, (r + 1) * tile)
            conv = done[j, at, :].astype(F32)
            hidden[at, cols] = (
                gate[at, cols] * (conv + skip[:, cols] * signal[at, cols])
            ).astype(BF)

    for k in range(1, seqs):
        signal_copy(k).wait_send()
        back_copy(k).wait_send()

    @pl.when(has_next)
    def _():
        halo.wait_send()


def scatter_kernel(
    chans, hidden, weight, out,
    cout, cin, yout, yin, zout, upin, downin,
    csend, crecv, ysend, yrecv, zsend, urecv, drecv,
):
    me, zi, yi, ci, far = position(chans)
    core, side, up, down = chan_peers(chans)
    rows, width = out.shape
    has_up, has_down = zi < far - 1, zi > 0
    greet([(core, None), (side, None), (up, has_up), (down, has_down)])

    tile = min(rows, 256)
    tiles = rows // tile

    def term(z, y, c, at):
        ident = z * 4 + y * 2 + c
        cols = pl.ds(pl.multiple_of(ident * width, width), width)
        return dot(hidden[at, :], weight[:, cols])

    def each_tile(do):
        @pl.loop(0, tiles)
        def _(r):
            do(pl.ds(pl.multiple_of(r * tile, tile), tile))

    def core_copy(y, z):
        return remote(cout.at[y * far + z], cin.at[y * far + z], csend.at[y * far + z], crecv.at[y * far + z], core)

    def side_copy(z):
        return remote(yout.at[z], yin.at[z], ysend.at[z], yrecv.at[z], side)

    def up_copy(z):
        return remote(zout.at[z], upin.at[z], zsend.at[z], urecv.at[z], up)

    def down_copy(z):
        return remote(zout.at[z], downin.at[z], zsend.at[z], drecv.at[z], down)

    def far_first(do):
        @pl.loop(0, far)
        def _(s):
            d = far - 1 - s

            @pl.when(zi + d < far)
            def _():
                do(zi + d)

            @pl.when(jnp.logical_and(zi - d >= 0, d > 0))
            def _():
                do(zi - d)

    def to_core(y):
        def go(z):
            def tiled(at):
                cout[y * far + z, at, :] = term(z, y, 1 - ci, at).astype(BF)

            each_tile(tiled)
            core_copy(y, z).start()

        return go

    def to_side(z):
        core_copy(1 - yi, z).wait_recv()

        def tiled(at):
            total = term(z, 1 - yi, ci, at) + cin[(1 - yi) * far + z, at, :].astype(F32)
            yout[z, at, :] = total.astype(BF)

        each_tile(tiled)
        side_copy(z).start()

    def total(z, at):
        return (
            term(z, yi, ci, at)
            + cin[yi * far + z, at, :].astype(F32)
            + yin[z, at, :].astype(F32)
        )

    def pass_on(z, arrived, land, copy, onward):
        core_copy(yi, z).wait_recv()
        side_copy(z).wait_recv()

        @pl.when(arrived)
        def _():
            onward(z).wait_recv()

            def tiled(at):
                zout[z, at, :] = (total(z, at) + land[z, at, :].astype(F32)).astype(BF)

            each_tile(tiled)

        @pl.when(jnp.logical_not(arrived))
        def _():
            def tiled(at):
                zout[z, at, :] = total(z, at).astype(BF)

            each_tile(tiled)

        copy(z).start()

    far_first(to_core(1 - yi))
    far_first(to_side)
    far_first(to_core(yi))

    @pl.loop(0, far - 1)
    def _(s):
        d = far - 1 - s

        @pl.when(zi + d < far)
        def _():
            pass_on(zi + d, has_down, upin, up_copy, up_copy)

        @pl.when(zi - d >= 0)
        def _():
            pass_on(zi - d, has_up, downin, down_copy, down_copy)

    core_copy(yi, zi).wait_recv()
    side_copy(zi).wait_recv()

    @pl.when(has_down)
    def _():
        up_copy(zi).wait_recv()

    @pl.when(has_up)
    def _():
        down_copy(zi).wait_recv()

    def finish(at):
        whole = total(zi, at)
        both = jnp.logical_and(has_down, has_up)

        @pl.when(both)
        def _():
            out[at, :] = (whole + upin[zi, at, :].astype(F32) + downin[zi, at, :].astype(F32)).astype(BF)

        @pl.when(jnp.logical_and(has_down, jnp.logical_not(has_up)))
        def _():
            out[at, :] = (whole + upin[zi, at, :].astype(F32)).astype(BF)

        @pl.when(jnp.logical_and(has_up, jnp.logical_not(has_down)))
        def _():
            out[at, :] = (whole + downin[zi, at, :].astype(F32)).astype(BF)

    each_tile(finish)

    @pl.loop(0, far)
    def _(z):
        core_copy(0, z).wait_send()
        core_copy(1, z).wait_send()
        side_copy(z).wait_send()

        @pl.when(z > zi)
        def _():
            up_copy(z).wait_send()

        @pl.when(z < zi)
        def _():
            down_copy(z).wait_send()


def call(kernel, out_shape, arity, scratch, ident):
    vmem = pl.BlockSpec(memory_space=pltpu.VMEM)
    many = isinstance(out_shape, (list, tuple))
    return pl.pallas_call(
        kernel,
        out_shape=out_shape,
        in_specs=[vmem] * arity,
        out_specs=[vmem] * len(out_shape) if many else vmem,
        scratch_shapes=scratch,
        compiler_params=pltpu.CompilerParams(
            collective_id=ident, has_side_effects=True, vmem_limit_bytes=50 * 2**20
        ),
    )


def body(seqs, chans, tokens, in_weight, short_taps, filter_taps, skip_gain, out_weight):
    rows, width = tokens.shape
    chan = in_weight.shape[2]
    far = chans // 4
    block = min(256, rows)
    count = seqs * rows // block
    narrow = chan // seqs
    dma = pltpu.SemaphoreType.DMA
    vm = pltpu.VMEM
    shape = jax.ShapeDtypeStruct
    flat_weight = in_weight.reshape(in_weight.shape[0], 3 * chan)
    fwd = jnp.asarray(forward_matrix(block))
    inv = jnp.asarray(inverse_matrix(block))
    projected, window = call(
        functools.partial(gather_kernel, seqs, chans),
        [shape((rows, 3 * chan), BF), shape((count, 2 * block, narrow), F32)],
        4,
        [
            vm((chans, rows, width), BF), vm((rows, 3 * chan), F32),
            vm((seqs, rows, narrow), F32), vm((seqs, rows, narrow), F32),
            vm((count, 2 * block, narrow), F32),
            dma((2, far)), dma((far,)), dma((far,)), dma((far,)),
            dma((2 * far,)), dma((2 * far,)), dma((seqs,)), dma((seqs,)),
        ],
        0,
    )(tokens, flat_weight, filter_taps, fwd)
    hidden = call(
        functools.partial(mix_kernel, seqs),
        shape((rows, chan), BF),
        6,
        [
            vm((HALO + rows, 3 * chan), F32), vm((HALO, 3 * chan), BF),
            vm((rows, chan), F32), vm((rows, chan), F32),
            vm((seqs, rows, narrow), BF), vm((seqs, rows, narrow), BF),
            vm((count, 2 * block, narrow), F32), vm((count, 2 * block, narrow), F32),
            vm((seqs, rows, narrow), BF), vm((seqs, rows, narrow), BF),
            dma, dma, dma((seqs,)), dma((seqs,)), dma((seqs,)), dma((seqs,)),
        ],
        1,
    )(projected, short_taps.reshape(9, chan), skip_gain.reshape(1, chan), fwd, inv, window)
    return call(
        functools.partial(scatter_kernel, chans),
        shape((rows, width), BF),
        2,
        [
            vm((2 * far, rows, width), BF), vm((2 * far, rows, width), BF),
            vm((far, rows, width), BF), vm((far, rows, width), BF),
            vm((far, rows, width), BF), vm((far, rows, width), BF), vm((far, rows, width), BF),
            dma((2 * far,)), dma((2 * far,)), dma((far,)), dma((far,)),
            dma((far,)), dma((far,)), dma((far,)),
        ],
        2,
    )(hidden, out_weight)


def solution(mesh):
    in_specs = (
        P("seq", "chan"),
        P(None, None, "chan"),
        P(None, None, "chan"),
        P("seq", "chan"),
        P("chan"),
        P("chan", None),
    )
    out_specs = P("seq", "chan")
    run = functools.partial(body, mesh.shape["seq"], mesh.shape["chan"])
    return jax.shard_map(run, mesh=mesh, in_specs=in_specs, out_specs=out_specs, check_vma=False)
```
